256 devices in a mesh: section: 4 (over x), dp: 32 (over y, z), tensor: 2 (over core).
Axes of the slice: x: 4, y: 4, z: 8, core: 2. Of those that a mesh axis runs over, the one named last changes fastest.
Arguments:
- activations: bfloat16 [4, 16384, 12288], P('section', 'dp'), may hold values from -600 to 600
- cotangent: bfloat16 [4, 16384, 1024], P('section', 'dp', 'tensor'), may hold values from -3.59375 to 3.59375
- params: float32 [4, 12288, 1024], P('section', 'dp', 'tensor'), may hold values from -4 to 4
- first_moment: float32 [4, 12288, 1024], P('section', 'dp', 'tensor'), may hold values from -0.6 to 0.6
- second_moment: float32 [4, 12288, 1024], P('section', 'dp', 'tensor'), may hold values from 0.002 to 0.02
- step_counts: int32 [4], P('section'), may hold values from 1 to 8
Outputs:
- new_params: float32 [4, 12288, 1024], P('section', 'dp', 'tensor')
- new_first: float32 [4, 12288, 1024], P('section', 'dp', 'tensor')
- new_second: float32 [4, 12288, 1024], P('section', 'dp', 'tensor')
The draws below stay inside these ranges and needn't reach their ends.
All inputs are finite; a program needn't handle non-finite values.
Results may differ from the reference program's by a relative error of at most 0.0003.
Values may be sent and summed in bfloat16 or wider, within the bound.
A program may use at most 128 MiB of HBM per device.

```python
import math
import jax
import jax.numpy as jnp
from jax import lax

D = 12288
TOK_DEV = 512
ROWS = 1024
TOKENS = 16384
N_SECTION = 4
N_DP = 32


def draw_activations(key, part):
    key = jax.random.fold_in(key, 11)
    keys = jax.random.split(key, 3)
    feature = jnp.arange(D, dtype=jnp.float32)
    ramp = 1.0 + feature / D
    rough = jnp.exp(jax.random.uniform(keys[0], (D,), jnp.float32, 0.0, math.log(6.0)))
    order = jax.random.permutation(keys[2], N_DP)
    token_block = jnp.arange(TOKENS) // TOK_DEV
    feature_block = jnp.arange(D) // (D // N_DP)
    spike = jnp.where(order[token_block][:, None] == feature_block[None, :], 3.0, 1.0)
    noise = jnp.clip(jax.random.normal(keys[1], (N_SECTION, TOKENS, D), jnp.float32), -6.0, 6.0)
    return (noise * spike[None] * (ramp * rough)[None, None, :]).astype(jnp.bfloat16)


def draw_cotangent(key, part):
    key = jax.random.fold_in(key, 23)
    keys = jax.random.split(key, 2)
    column = jnp.arange(ROWS, dtype=jnp.float32)
    ramp = 1.0 + 3.0 * column / ROWS
    rough = jnp.exp(jax.random.uniform(keys[0], (ROWS,), jnp.float32, 0.0, math.log(4.0)))
    section_ramp = 1.0 + jnp.arange(N_SECTION, dtype=jnp.float32) / max(N_SECTION - 1, 1)
    noise = jnp.clip(jax.random.normal(keys[1], (N_SECTION, TOKENS, ROWS), jnp.float32), -6.0, 6.0)
    scaled = noise * (ramp * rough)[None, None, :] * section_ramp[:, None, None] / math.sqrt(TOKENS)
    return scaled.astype(jnp.bfloat16)


def touch_ends(entries, rng, low, top_value):
    longest = entries.shape.index(max(entries.shape))
    spots = []
    for shift in (0, 1):
        where = [jax.random.randint(jax.random.fold_in(rng, axis), (), 0, length) for axis, length in enumerate(entries.shape)]
        where[longest] = (where[longest] + shift) % entries.shape[longest]
        spots.append(tuple(where))
    return entries.at[spots[0]].set(low).at[spots[1]].set(top_value)


def shard_levels(key, dims, cuts, least, largest):
    def one(dim, blocks):
        steps = jax.random.uniform(jax.random.fold_in(jax.random.fold_in(key, 6), dim), (blocks,), jnp.float32, least / len(cuts), largest / len(cuts))
        return jnp.repeat(jnp.exp(steps), dims[dim] // blocks).reshape((-1,) + (1,) * (len(dims) - dim - 1))

    factor_of = one(*cuts[0])
    for cut in cuts[1:]:
        factor_of = factor_of * one(*cut)
    return factor_of


def gaussian(rng, dims, spread, bound, cuts=(), kind=jnp.bfloat16):
    drawn = spread * jax.random.normal(rng, dims, jnp.float32)
    if cuts:
        drawn = drawn * shard_levels(rng, dims, cuts, -0.22, 0.18)
    return jnp.clip(drawn, -bound, bound).astype(kind)


def setup_inputs(seed: int = 0) -> dict:
    arg_keys = jax.random.split(jax.random.key(seed), 7)
    return {
        "activations": draw_activations(jax.random.fold_in(arg_keys[6], 71), 0),
        "cotangent": draw_cotangent(jax.random.fold_in(arg_keys[6], 71), 0),
        "params": gaussian(arg_keys[2], (N_SECTION, D, ROWS), 1.0, 4.0, ((0, 4), (1, 32), (2, 2)), jnp.float32),
        "first_moment": gaussian(arg_keys[3], (N_SECTION, D, ROWS), 0.1, 0.6, ((0, 4), (1, 32), (2, 2)), jnp.float32),
        "second_moment": jnp.clip(jnp.exp(math.log(0.02) - 2.30258502 * jax.random.uniform(arg_keys[4], (N_SECTION, D, ROWS), jnp.float32) ** shard_levels(arg_keys[4], (N_SECTION, D, ROWS), ((0, 4), (1, 32), (2, 2)), -0.2, 0.2)), 0.002, 0.02),
        "step_counts": touch_ends(jax.random.randint(arg_keys[5], (N_SECTION,), 1, 9), jax.random.fold_in(arg_keys[5], 1), 1, 8).astype(jnp.int32),
    }


beta_one = 0.9
beta_two = 0.95
learn_rate = 0.05
decay_rate = 0.1
epsilon = 1e-08
clip_scale = 0.25

def section_gradient(section_pair):
    layer_input, out_grads = section_pair
    return jnp.dot(layer_input.T, out_grads, preferred_element_type=jnp.float32)

def reference(activations, cotangent, params, first_moment, second_moment, step_counts):
    gradient = lax.map(section_gradient, (activations, cotangent))
    global_sq = jnp.sum(gradient * gradient)
    threshold = clip_scale * math.sqrt(N_SECTION * D * ROWS)
    clip_factor = jnp.minimum(1.0, threshold / jnp.sqrt(global_sq))
    clipped = clip_factor * gradient
    new_first = beta_one * first_moment + (1.0 - beta_one) * clipped
    new_second = beta_two * second_moment + (1.0 - beta_two) * clipped * clipped
    steps_now = step_counts.astype(jnp.float32)[:, None, None]
    first_fix = 1.0 - jnp.power(jnp.float32(beta_one), steps_now)
    second_fix = 1.0 - jnp.power(jnp.float32(beta_two), steps_now)
    update = new_first / first_fix / (jnp.sqrt(new_second / second_fix) + epsilon)
    new_params = params * (1.0 - learn_rate * decay_rate) - learn_rate * update
    return (new_params, new_first, new_second)
```

```python
import functools
import math

import jax
import jax.numpy as jnp
from jax import lax
from jax.experimental import pallas as pl
from jax.experimental.pallas import tpu as pltpu
from jax.sharding import PartitionSpec as P

beta_one = 0.9
beta_two = 0.95
learn_rate = 0.05
decay_rate = 0.1
epsilon = 1e-08
clip_scale = 0.25

MESH = pl.DeviceIdType.MESH
f32 = jnp.float32

NY, NZ, DB, UN, TOK = 4, 8, 384, 512, 512
RA, RB = 304, 208
HA, HB = (160, 144), (96, 112)
TILE = 16
LEVELS = 32766.0

O_AYH = 0
O_AYF = O_AYH + NZ * RA
O_AZH = O_AYF + 2 * NZ * RA
O_AZF = O_AZH + RA
O_BZH = O_AZF + 6 * RA
O_BZF = O_BZH + NY * RB
O_BYH = O_BZF + 6 * NY * RB
O_BYF = O_BYH + RB
ROWS_ALL = O_BYF + 2 * RB
N_PIECES = 76


def piece_ayh(dz, d):
    return dz * 2 + d, O_AYH + dz * RA + d * HA[0], HA[d]


def piece_ayf(dz, d):
    return 16 + dz * 2 + d, O_AYF + (dz * 2 + d) * RA, RA


def piece_azh(d):
    return 32 + d, O_AZH + d * HA[0], HA[d]


def piece_azf(j, d):
    return 34 + (j - 1) * 2 + d, O_AZF + ((j - 1) * 2 + d) * RA, RA


def piece_bzh(dy, d):
    return 40 + dy * 2 + d, O_BZH + dy * RB + d * HB[0], HB[d]


def piece_bzf(dy, j, d):
    return 48 + dy * 6 + (j - 1) * 2 + d, O_BZF + (dy * 6 + (j - 1) * 2 + d) * RB, RB


def piece_byh(d):
    return 72 + d, O_BYH + d * HB[0], HB[d]


def piece_byf(d):
    return 74 + d, O_BYF + d * RB, RB


SCHEDULE = [20, 276, 284, 21, 268, 19, 260, 307, 92, 341, 44, 315, 349, 93, 43, 299, 333, 91, 370, 374, 45, 291, 382, 22, 378, 366, 18, 362, 325, 17, 94, 46, 100, 367, 377, 90, 42, 375, 369, 89, 131, 165, 41, 361, 383, 23, 354, 16, 358, 400, 194, 198, 95, 47, 353, 359, 88, 40, 193, 199, 472, 424, 480, 224]


def firsts(schedule):
    seen, marks = [], []
    for code in schedule:
        block = code % 32
        marks.append(0 if block in seen else len(seen) + 1)
        if block not in seen:
            seen.append(block)
    return seen, marks


BLOCK_ORDER, FIRST_USE = firsts(SCHEDULE)


def pick(table, index):
    value = jnp.int32(table[0])
    for place in range(1, len(table)):
        value = jnp.where(index == place, jnp.int32(table[place]), value)
    return value


PEERS_C = [(0, 0, 0, 1)]
PEERS_XY = [(i, j, 0, 0) for i in range(4) for j in range(4) if i or j]
PEERS_Z = [(0, 0, i, 0) for i in range(1, 8)]


def kernel(act_ref, cot_ref, grad_ref, sq_ref, act, cot_t, total, final, send, recv, send_scale, recv_scale,
           sq_vec, sq_c, sq_xy, sq_z, sq_out, act_sem, send_sem, recv_sem, send_scale_sem, recv_scale_sem,
           norm_send_sem, norm_recv_sem):
    section = lax.axis_index("section")
    dp = lax.axis_index("dp")
    core = lax.axis_index("tensor")
    y, z = lax.div(dp, NZ), lax.rem(dp, NZ)

    def peer(dx, dy, dz, dc):
        return (
            lax.rem(section + dx, 4),
            lax.rem(y + dy, NY) * NZ + lax.rem(z + dz, NZ),
            lax.rem(core + dc, 2),
        )

    def block_columns(dy, dz):
        block = lax.rem(y + dy, NY) * NZ + lax.rem(z + dz, NZ)
        return pl.ds(pl.multiple_of(block * DB, DB), DB)

    barrier = pltpu.get_barrier_semaphore()
    peers = PEERS_C + PEERS_XY + PEERS_Z
    for offset in peers:
        pl.semaphore_signal(barrier, inc=1, device_id=peer(*offset), device_id_type=MESH)

    def act_copy(order, offset):
        columns = block_columns(offset // NZ, offset % NZ)
        return pltpu.make_async_copy(act_ref.at[0, :, columns], act.at[:, columns], act_sem.at[order])

    @pl.loop(0, NY * NZ)
    def _(order):
        act_copy(order, pick(BLOCK_ORDER, order)).start()

    cot_t[...] = cot_ref[0].T
    pl.semaphore_wait(barrier, len(peers))

    def rows_of(offset, count):
        return pl.ds(pl.multiple_of(offset, TILE), count)

    def copies(piece, to):
        number, offset, count = piece
        rows = rows_of(offset, count)
        data = pltpu.make_async_remote_copy(
            src_ref=send.at[rows], dst_ref=recv.at[rows], send_sem=send_sem.at[number], recv_sem=recv_sem.at[number],
            device_id=to, device_id_type=MESH)
        scale = pltpu.make_async_remote_copy(
            src_ref=send_scale.at[number], dst_ref=recv_scale.at[number], send_sem=send_scale_sem.at[number],
            recv_sem=recv_scale_sem.at[number], device_id=to, device_id_type=MESH)
        return data, scale

    nowhere = peer(0, 0, 0, 1)

    def step(in_a, dy, dz, arrivals, departures):
        start, count = (0, RA) if in_a else (RA, RB)
        total[pl.ds(0, count)] = jnp.dot(
            cot_t[pl.ds(start, count)], act[:, block_columns(dy, dz)], preferred_element_type=f32)
        scales = []
        for piece, _ in arrivals:
            for copy in copies(piece, nowhere):
                copy.wait_recv()
            scales.append(recv_scale[piece[0]])
        top = jnp.zeros((8, DB), f32)
        for row in range(0, count, TILE):
            value = total[pl.ds(row, TILE)]
            for (piece, first), scale in zip(arrivals, scales):
                if first <= row < first + piece[2]:
                    code = recv[rows_of(piece[1] + (row - first), TILE)]
                    value = value + code.astype(jnp.int32).astype(f32) * scale
            if departures:
                if arrivals:
                    total[pl.ds(row, TILE)] = value
                size = jnp.abs(value)
                top = jnp.maximum(top, jnp.maximum(size[:8], size[8:]))
            else:
                final[pl.ds(start + row, TILE)] = value
                square = value * value
                top = top + (square[:8] + square[8:])
        if not departures:
            sq_vec[0 if in_a else 1] = top
            return
        top = jnp.maximum(jnp.max(top, axis=0, keepdims=True), 1e-30)
        inverse = LEVELS / top
        for piece, first, to in departures:
            number, offset, size = piece
            send_scale[number] = top * (1.0 / LEVELS)
            for row in range(0, size, TILE):
                code = jnp.round(total[pl.ds(first + row, TILE)] * inverse)
                send[rows_of(offset + row, TILE)] = code.astype(jnp.int32).astype(jnp.int16)
            for copy in copies(piece, to):
                copy.start()

    y_peer = (peer(0, 1, 0, 0), peer(0, NY - 1, 0, 0))
    z_peer = (peer(0, 0, 1, 0), peer(0, 0, NZ - 1, 0))

    def z_toward(d):
        return peer(0, 0, 1 + (NZ - 2) * d, 0)

    @pl.loop(0, len(SCHEDULE))
    def _(index):
        code = pick(SCHEDULE, index)
        first_use = pick(FIRST_USE, index)
        kind, offset = lax.div(code, 32), lax.rem(code, 32)
        dy, dz = lax.div(offset, NZ), lax.rem(offset, NZ)

        @pl.when(first_use > 0)
        def _():
            act_copy(first_use - 1, offset).wait()

        def when(value):
            return pl.when(kind == value)

        @when(0)
        def _():
            step(True, dy, dz, [], [
                (piece_ayh(dz, 0), 0, y_peer[0]), (piece_ayh(dz, 1), HA[0], y_peer[1])])

        for d in (0, 1):
            @when(1 + d)
            def _(d=d):
                step(True, dy, dz, [(piece_ayh(dz, d), d * HA[0])], [(piece_ayf(dz, d), 0, y_peer[d])])

        def summed_over_y():
            return [(piece_ayf(dz, 0), 0), (piece_ayf(dz, 1), 0)]

        @when(3)
        def _():
            step(True, dy, dz, summed_over_y(), [
                (piece_azh(0), 0, z_peer[0]), (piece_azh(1), HA[0], z_peer[1])])

        for d in (0, 1):
            @when(4 + d)
            def _(d=d):
                step(True, dy, dz, summed_over_y() + [(piece_azh(d), d * HA[0])], [(piece_azf(3, d), 0, z_peer[d])])

        toward = (dz > NZ // 2).astype(jnp.int32)
        hops = jnp.where(dz > NZ // 2, NZ - dz, dz)

        @when(6)
        def _():
            step(True, dy, dz, summed_over_y() + [(piece_azf(hops + 1, toward), 0)],
                 [(piece_azf(hops, toward), 0, z_toward(toward))])

        @when(7)
        def _():
            step(True, dy, dz, summed_over_y() + [(piece_azf(1, 0), 0), (piece_azf(1, 1), 0)], [])

        @when(8)
        def _():
            step(False, dy, dz, [], [
                (piece_bzh(dy, 0), 0, z_peer[0]), (piece_bzh(dy, 1), HB[0], z_peer[1])])

        for d in (0, 1):
            @when(9 + d)
            def _(d=d):
                step(False, dy, dz, [(piece_bzh(dy, d), d * HB[0])], [(piece_bzf(dy, 3, d), 0, z_peer[d])])

        @when(11)
        def _():
            step(False, dy, dz, [(piece_bzf(dy, hops + 1, toward), 0)],
                 [(piece_bzf(dy, hops, toward), 0, z_toward(toward))])

        def summed_over_z():
            return [(piece_bzf(dy, 1, 0), 0), (piece_bzf(dy, 1, 1), 0)]

        @when(12)
        def _():
            step(False, dy, dz, summed_over_z(), [
                (piece_byh(0), 0, y_peer[0]), (piece_byh(1), HB[0], y_peer[1])])

        for d in (0, 1):
            @when(13 + d)
            def _(d=d):
                step(False, dy, dz, summed_over_z() + [(piece_byh(d), d * HB[0])], [(piece_byf(d), 0, y_peer[d])])

        @when(15)
        def _():
            step(False, dy, dz, summed_over_z() + [(piece_byf(0), 0), (piece_byf(1), 0)], [])

    lanes = jnp.sum(sq_vec[0] + sq_vec[1], axis=0, keepdims=True)
    value = lanes[:, :128] + lanes[:, 128:256] + lanes[:, 256:]
    place = 0
    waiting = []
    for stage, (offsets, slots) in enumerate(((PEERS_C, sq_c), (PEERS_XY, sq_xy), (PEERS_Z, sq_z))):
        sq_out[stage] = value
        exchange = []
        for slot, offset in enumerate(offsets):
            copy = pltpu.make_async_remote_copy(
                src_ref=sq_out.at[stage], dst_ref=slots.at[slot], send_sem=norm_send_sem.at[place],
                recv_sem=norm_recv_sem.at[place], device_id=peer(*offset), device_id_type=MESH)
            copy.start()
            exchange.append(copy)
            place += 1
        if stage == 1:
            grad_ref[...] = final[...].T
        for copy in exchange:
            copy.wait_recv()
        for slot in range(len(offsets)):
            value = value + slots[slot]
        waiting += exchange
    sq_ref[...] = jnp.broadcast_to(jnp.sum(value, axis=1, keepdims=True), (8, 128))

    for copy in waiting:
        copy.wait_send()

    def sent(count, piece):
        @pl.loop(0, count)
        def _(index):
            for copy in copies(piece(index), nowhere):
                copy.wait_send()

    for d in (0, 1):
        sent(NZ, lambda i, d=d: piece_ayh(i, d))
        sent(NZ, lambda i, d=d: piece_ayf(i, d))
        sent(1, lambda i, d=d: piece_azh(d))
        sent(3, lambda i, d=d: piece_azf(i + 1, d))
        sent(NY, lambda i, d=d: piece_bzh(i, d))
        for dy in range(NY):
            sent(3, lambda i, d=d, dy=dy: piece_bzf(dy, i + 1, d))
        sent(1, lambda i, d=d: piece_byh(d))
        sent(1, lambda i, d=d: piece_byf(d))


def reduced_gradient(activations, cotangent):
    dma = pltpu.SemaphoreType.DMA
    return pl.pallas_call(
        kernel,
        out_shape=(jax.ShapeDtypeStruct((DB, UN), f32), jax.ShapeDtypeStruct((8, 128), f32)),
        in_specs=[pl.BlockSpec(memory_space=pl.ANY), pl.BlockSpec(memory_space=pltpu.VMEM)],
        out_specs=[pl.BlockSpec(memory_space=pltpu.VMEM)] * 2,
        scratch_shapes=[
            pltpu.VMEM((TOK, NY * NZ * DB), jnp.bfloat16),
            pltpu.VMEM((UN, TOK), jnp.bfloat16),
            pltpu.VMEM((RA, DB), f32),
            pltpu.VMEM((UN, DB), f32),
            pltpu.VMEM((ROWS_ALL, DB), jnp.int16),
            pltpu.VMEM((ROWS_ALL, DB), jnp.int16),
            pltpu.VMEM((N_PIECES, 1, DB), f32),
            pltpu.VMEM((N_PIECES, 1, DB), f32),
            pltpu.VMEM((2, 8, DB), f32),
            pltpu.VMEM((1, 1, 128), f32),
            pltpu.VMEM((15, 1, 128), f32),
            pltpu.VMEM((7, 1, 128), f32),
            pltpu.VMEM((3, 1, 128), f32),
            dma((NY * NZ,)),
            dma((N_PIECES,)),
            dma((N_PIECES,)),
            dma((N_PIECES,)),
            dma((N_PIECES,)),
            dma((23,)),
            dma((23,)),
        ],
        compiler_params=pltpu.CompilerParams(collective_id=0, has_side_effects=True, vmem_limit_bytes=56 << 20),
    )(activations, cotangent)


def body(activations, cotangent, params, first_moment, second_moment, step_counts):
    feature_count = activations.shape[2]
    unit_count = cotangent.shape[2]
    grad_shard, squares = reduced_gradient(activations, cotangent)
    global_sq = squares[0, 0]
    threshold = clip_scale * math.sqrt(
        lax.axis_size("section") * feature_count * unit_count * lax.axis_size("tensor")
    )
    clip_factor = jnp.minimum(1.0, threshold / jnp.sqrt(global_sq))
    clipped = clip_factor * grad_shard[None]
    new_first = beta_one * first_moment + (1.0 - beta_one) * clipped
    new_second = beta_two * second_moment + (1.0 - beta_two) * clipped * clipped
    steps_now = step_counts[0].astype(jnp.float32)
    first_fix = 1.0 - jnp.power(jnp.float32(beta_one), steps_now)
    second_fix = 1.0 - jnp.power(jnp.float32(beta_two), steps_now)
    update = new_first / first_fix / (jnp.sqrt(new_second / second_fix) + epsilon)
    new_params = params * (1.0 - learn_rate * decay_rate) - learn_rate * update
    return (new_params, new_first, new_second)


def solution(mesh):
    in_specs = (
        P("section", "dp", None),
        P("section", "dp", "tensor"),
        P("section", "dp", "tensor"),
        P("section", "dp", "tensor"),
        P("section", "dp", "tensor"),
        P("section"),
    )
    out_specs = (
        P("section", "dp", "tensor"),
        P("section", "dp", "tensor"),
        P("section", "dp", "tensor"),
    )
    return jax.shard_map(body, mesh=mesh, in_specs=in_specs, out_specs=out_specs, check_vma=False)
```

```python
import functools
import math

import jax
import jax.numpy as jnp
from jax import lax
from jax.experimental import pallas as pl
from jax.experimental.pallas import tpu as pltpu
from jax.sharding import PartitionSpec as P

beta_one = 0.9
beta_two = 0.95
learn_rate = 0.05
decay_rate = 0.1
epsilon = 1e-08
clip_scale = 0.25

MESH = pl.DeviceIdType.MESH
f32 = jnp.float32

NY, NZ, DB, UN, TOK = 4, 8, 384, 512, 512
RA, RB = 304, 208
HA, HB = (160, 144), (96, 112)
TILE = 16
LEVELS = 32766.0

O_AYH = 0
O_AYF = O_AYH + NZ * RA
O_AZH = O_AYF + 2 * NZ * RA
O_AZF = O_AZH + RA
O_BZH = O_AZF + 6 * RA
O_BZF = O_BZH + NY * RB
O_BYH = O_BZF + 6 * NY * RB
O_BYF = O_BYH + RB
ROWS_ALL = O_BYF + 2 * RB
N_PIECES = 76


def piece_ayh(dz, d):
    return dz * 2 + d, O_AYH + dz * RA + d * HA[0], HA[d]


def piece_ayf(dz, d):
    return 16 + dz * 2 + d, O_AYF + (dz * 2 + d) * RA, RA


def piece_azh(d):
    return 32 + d, O_AZH + d * HA[0], HA[d]


def piece_azf(j, d):
    return 34 + (j - 1) * 2 + d, O_AZF + ((j - 1) * 2 + d) * RA, RA


def piece_bzh(dy, d):
    return 40 + dy * 2 + d, O_BZH + dy * RB + d * HB[0], HB[d]


def piece_bzf(dy, j, d):
    return 48 + dy * 6 + (j - 1) * 2 + d, O_BZF + (dy * 6 + (j - 1) * 2 + d) * RB, RB


def piece_byh(d):
    return 72 + d, O_BYH + d * HB[0], HB[d]


def piece_byf(d):
    return 74 + d, O_BYF + d * RB, RB


SCHEDULE = [20, 268, 19, 276, 260, 18, 284, 22, 299, 333, 21, 291, 341, 44, 92, 307, 349, 23, 315, 93, 366, 45, 362, 374, 43, 100, 91, 354, 378, 325, 17, 367, 94, 46, 370, 165, 42, 131, 90, 47, 375, 377, 95, 369, 382, 16, 89, 198, 194, 358, 41, 383, 361, 400, 353, 88, 40, 199, 193, 424, 359, 472, 224, 480]


def firsts(schedule):
    seen, marks = [], []
    for code in schedule:
        block = code % 32
        marks.append(0 if block in seen else len(seen) + 1)
        if block not in seen:
            seen.append(block)
    return seen, marks


BLOCK_ORDER, FIRST_USE = firsts(SCHEDULE)


def pick(table, index):
    values = [jnp.int32(entry) for entry in table]
    step = 1
    while len(values) > 1:
        odd = lax.rem(lax.div(index, step), 2) == 1
        values = [jnp.where(odd, b, a) for a, b in zip(values[::2], values[1::2], strict=True)]
        step *= 2
    return values[0]


EARLY = 2


PEERS_C = [(0, 0, 0, 1)]
PEERS_XY = [(i, j, 0, 0) for i in range(4) for j in range(4) if i or j]
PEERS_Z = [(0, 0, i, 0) for i in range(1, 8)]


def kernel(act_ref, cot_hbm, grad_ref, clip_ref, act, cot_t, total, final, send, recv, send_scale, recv_scale,
           sq_vec, sq_c, sq_xy, sq_z, sq_out, act_sem, send_sem, recv_sem, send_scale_sem, recv_scale_sem,
           norm_send_sem, norm_recv_sem, cot_ref, cot_sem):
    section = lax.axis_index("section")
    dp = lax.axis_index("dp")
    core = lax.axis_index("tensor")
    y, z = lax.div(dp, NZ), lax.rem(dp, NZ)

    def peer(dx, dy, dz, dc):
        return (
            lax.rem(section + dx, 4),
            lax.rem(y + dy, NY) * NZ + lax.rem(z + dz, NZ),
            lax.rem(core + dc, 2),
        )

    def block_columns(dy, dz):
        block = lax.rem(y + dy, NY) * NZ + lax.rem(z + dz, NZ)
        return pl.ds(pl.multiple_of(block * DB, DB), DB)

    barrier = pltpu.get_barrier_semaphore()
    peers = PEERS_C + PEERS_XY + PEERS_Z
    for offset in peers:
        pl.semaphore_signal(barrier, inc=1, device_id=peer(*offset), device_id_type=MESH)

    cot_copy = pltpu.make_async_copy(cot_hbm.at[0], cot_ref, cot_sem)
    cot_copy.start()

    def act_copy(order, offset):
        columns = block_columns(offset // NZ, offset % NZ)
        return pltpu.make_async_copy(act_ref.at[0, :, columns], act.at[:, columns], act_sem.at[order])

    @pl.loop(0, NY * NZ)
    def _(order):
        act_copy(order, pick(BLOCK_ORDER, order)).start()

    cot_copy.wait()
    cot_t[...] = cot_ref[...].T
    def rows_of(offset, count):
        return pl.ds(pl.multiple_of(offset, TILE), count)

    def copies(piece, to):
        number, offset, count = piece
        rows = rows_of(offset, count)
        data = pltpu.make_async_remote_copy(
            src_ref=send.at[rows], dst_ref=recv.at[rows], send_sem=send_sem.at[number], recv_sem=recv_sem.at[number],
            device_id=to, device_id_type=MESH)
        scale = pltpu.make_async_remote_copy(
            src_ref=send_scale.at[number], dst_ref=recv_scale.at[number], send_sem=send_scale_sem.at[number],
            recv_sem=recv_scale_sem.at[number], device_id=to, device_id_type=MESH)
        return data, scale

    nowhere = peer(0, 0, 0, 1)

    def send_off(departures):
        for piece, _, to in departures:
            for copy in copies(piece, to):
                copy.start()

    def step(index, in_a, dy, dz, arrivals, departures):
        start, count = (0, RA) if in_a else (RA, RB)
        total[pl.ds(0, count)] = jnp.dot(
            cot_t[pl.ds(start, count)], act[:, block_columns(dy, dz)], preferred_element_type=f32)
        scales = []
        for piece, _ in arrivals:
            for copy in copies(piece, nowhere):
                copy.wait_recv()
            scales.append(recv_scale[piece[0]])
        top = jnp.zeros((8, DB), f32)
        for row in range(0, count, TILE):
            value = total[pl.ds(row, TILE)]
            for (piece, first), scale in zip(arrivals, scales):
                if first <= row < first + piece[2]:
                    code = recv[rows_of(piece[1] + (row - first), TILE)]
                    value = value + code.astype(jnp.int32).astype(f32) * scale
            if departures:
                if arrivals:
                    total[pl.ds(row, TILE)] = value
                size = jnp.abs(value)
                top = jnp.maximum(top, jnp.maximum(size[:8], size[8:]))
            else:
                final[pl.ds(start + row, TILE)] = value
                square = value * value
                top = top + (square[:8] + square[8:])
        if not departures:
            sq_vec[0 if in_a else 1] = top
            return
        top = jnp.maximum(jnp.max(top, axis=0, keepdims=True), 1e-30)
        inverse = LEVELS / top
        for piece, first, to in departures:
            number, offset, size = piece
            send_scale[number] = top * (1.0 / LEVELS)
            for row in range(0, size, TILE):
                code = jnp.round(total[pl.ds(first + row, TILE)] * inverse)
                send[rows_of(offset + row, TILE)] = code.astype(jnp.int32).astype(jnp.int16)
        if arrivals:
            send_off(departures)
        else:
            pl.when(index >= EARLY)(lambda: send_off(departures))

    y_peer = (peer(0, 1, 0, 0), peer(0, NY - 1, 0, 0))
    z_peer = (peer(0, 0, 1, 0), peer(0, 0, NZ - 1, 0))

    def first_of_a(dz):
        return [(piece_ayh(dz, 0), 0, y_peer[0]), (piece_ayh(dz, 1), HA[0], y_peer[1])]

    def first_of_b(dy):
        return [(piece_bzh(dy, 0), 0, z_peer[0]), (piece_bzh(dy, 1), HB[0], z_peer[1])]

    def z_toward(d):
        return peer(0, 0, 1 + (NZ - 2) * d, 0)

    @pl.loop(0, len(SCHEDULE))
    def _(index):
        @pl.when(index == EARLY)
        def _():
            pl.semaphore_wait(barrier, len(peers))
            for early in SCHEDULE[:EARLY]:
                send_off(first_of_a(early % NZ) if early < 32 else first_of_b(early // NZ % NY))

        entry = pick([code * 64 + mark for code, mark in zip(SCHEDULE, FIRST_USE)], index)
        code, first_use = lax.div(entry, 64), lax.rem(entry, 64)
        kind, offset = lax.div(code, 32), lax.rem(code, 32)
        dy, dz = lax.div(offset, NZ), lax.rem(offset, NZ)

        @pl.when(first_use > 0)
        def _():
            act_copy(first_use - 1, offset).wait()

        kinds = {}

        def when(value):
            return functools.partial(kinds.__setitem__, value)

        @when(0)
        def _():
            step(index, True, dy, dz, [], first_of_a(dz))

        for d in (0, 1):
            @when(1 + d)
            def _(d=d):
                step(index, True, dy, dz, [(piece_ayh(dz, d), d * HA[0])], [(piece_ayf(dz, d), 0, y_peer[d])])

        def summed_over_y():
            return [(piece_ayf(dz, 0), 0), (piece_ayf(dz, 1), 0)]

        @when(3)
        def _():
            step(index, True, dy, dz, summed_over_y(), [
                (piece_azh(0), 0, z_peer[0]), (piece_azh(1), HA[0], z_peer[1])])

        for d in (0, 1):
            @when(4 + d)
            def _(d=d):
                step(index, True, dy, dz, summed_over_y() + [(piece_azh(d), d * HA[0])], [(piece_azf(3, d), 0, z_peer[d])])

        toward = (dz > NZ // 2).astype(jnp.int32)
        hops = jnp.where(dz > NZ // 2, NZ - dz, dz)

        @when(6)
        def _():
            step(index, True, dy, dz, summed_over_y() + [(piece_azf(hops + 1, toward), 0)],
                 [(piece_azf(hops, toward), 0, z_toward(toward))])

        @when(7)
        def _():
            step(index, True, dy, dz, summed_over_y() + [(piece_azf(1, 0), 0), (piece_azf(1, 1), 0)], [])

        @when(8)
        def _():
            step(index, False, dy, dz, [], first_of_b(dy))

        for d in (0, 1):
            @when(9 + d)
            def _(d=d):
                step(index, False, dy, dz, [(piece_bzh(dy, d), d * HB[0])], [(piece_bzf(dy, 3, d), 0, z_peer[d])])

        @when(11)
        def _():
            step(index, False, dy, dz, [(piece_bzf(dy, hops + 1, toward), 0)],
                 [(piece_bzf(dy, hops, toward), 0, z_toward(toward))])

        def summed_over_z():
            return [(piece_bzf(dy, 1, 0), 0), (piece_bzf(dy, 1, 1), 0)]

        @when(12)
        def _():
            step(index, False, dy, dz, summed_over_z(), [
                (piece_byh(0), 0, y_peer[0]), (piece_byh(1), HB[0], y_peer[1])])

        for d in (0, 1):
            @when(13 + d)
            def _(d=d):
                step(index, False, dy, dz, summed_over_z() + [(piece_byh(d), d * HB[0])], [(piece_byf(d), 0, y_peer[d])])

        @when(15)
        def _():
            step(index, False, dy, dz, summed_over_z() + [(piece_byf(0), 0), (piece_byf(1), 0)], [])

        def dispatch(low, high):
            if high - low == 1:
                if low in kinds:
                    kinds[low]()
                return
            middle = (low + high) // 2
            pl.when(kind < middle)(lambda: dispatch(low, middle))
            pl.when(kind >= middle)(lambda: dispatch(middle, high))

        dispatch(0, 16)

    def sent(count, piece):
        @pl.loop(0, count)
        def _(index):
            for copy in copies(piece(index), nowhere):
                copy.wait_send()
    def wait_for_sends():
        for d in (0, 1):
            sent(NZ, lambda i, d=d: piece_ayh(i, d))
            sent(NZ, lambda i, d=d: piece_ayf(i, d))
            sent(1, lambda i, d=d: piece_azh(d))
            sent(3, lambda i, d=d: piece_azf(i + 1, d))
            sent(NY, lambda i, d=d: piece_bzh(i, d))
            for dy in range(NY):
                sent(3, lambda i, d=d, dy=dy: piece_bzf(dy, i + 1, d))
            sent(1, lambda i, d=d: piece_byh(d))
            sent(1, lambda i, d=d: piece_byf(d))

    lanes = jnp.sum(sq_vec[0] + sq_vec[1], axis=0, keepdims=True)
    value = lanes[:, :128] + lanes[:, 128:256] + lanes[:, 256:]
    place = 0
    waiting = []
    for stage, (offsets, slots) in enumerate(((PEERS_C, sq_c), (PEERS_XY, sq_xy), (PEERS_Z, sq_z))):
        sq_out[stage] = value
        exchange = []
        for slot, offset in enumerate(offsets):
            copy = pltpu.make_async_remote_copy(
                src_ref=sq_out.at[stage], dst_ref=slots.at[slot], send_sem=norm_send_sem.at[place],
                recv_sem=norm_recv_sem.at[place], device_id=peer(*offset), device_id_type=MESH)
            copy.start()
            exchange.append(copy)
            place += 1
        if stage == 1:
            wait_for_sends()
        if stage == 2:
            grad_ref[...] = final[...].T
        for copy in exchange:
            copy.wait_recv()
        for slot in range(len(offsets)):
            value = value + slots[slot]
        waiting += exchange
    threshold = clip_scale * math.sqrt(4 * NY * NZ * DB * UN * 2)
    norm = jnp.sqrt(jnp.broadcast_to(jnp.sum(value, axis=1, keepdims=True), (1, UN)))
    clip_ref[...] = jnp.minimum(1.0, threshold / norm)

    for copy in waiting:
        copy.wait_send()


def reduced_gradient(activations, cotangent):
    dma = pltpu.SemaphoreType.DMA
    return pl.pallas_call(
        kernel,
        out_shape=(jax.ShapeDtypeStruct((DB, UN), f32), jax.ShapeDtypeStruct((1, UN), f32)),
        in_specs=[pl.BlockSpec(memory_space=pl.ANY), pl.BlockSpec(memory_space=pltpu.HBM)],
        out_specs=[pl.BlockSpec(memory_space=pltpu.VMEM)] * 2,
        scratch_shapes=[
            pltpu.VMEM((TOK, NY * NZ * DB), jnp.bfloat16),
            pltpu.VMEM((UN, TOK), jnp.bfloat16),
            pltpu.VMEM((RA, DB), f32),
            pltpu.VMEM((UN, DB), f32),
            pltpu.VMEM((ROWS_ALL, DB), jnp.int16),
            pltpu.VMEM((ROWS_ALL, DB), jnp.int16),
            pltpu.VMEM((N_PIECES, 1, DB), f32),
            pltpu.VMEM((N_PIECES, 1, DB), f32),
            pltpu.VMEM((2, 8, DB), f32),
            pltpu.VMEM((1, 1, 128), f32),
            pltpu.VMEM((15, 1, 128), f32),
            pltpu.VMEM((7, 1, 128), f32),
            pltpu.VMEM((3, 1, 128), f32),
            dma((NY * NZ,)),
            dma((N_PIECES,)),
            dma((N_PIECES,)),
            dma((N_PIECES,)),
            dma((N_PIECES,)),
            dma((23,)),
            dma((23,)),
            pltpu.VMEM((TOK, UN), jnp.bfloat16),
            dma(()),
        ],
        compiler_params=pltpu.CompilerParams(collective_id=0, has_side_effects=True, vmem_limit_bytes=46 << 20),
    )(activations, cotangent)


def update_kernel(grad_ref, clip_ref, count_ref, params_ref, first_ref, second_ref, new_params_ref, new_first_ref, new_second_ref):
    clip_factor = clip_ref[...]
    steps_now = jnp.full((1, UN), count_ref[0], jnp.int32)

    def power(base):
        result, base = jnp.ones((1, UN), f32), jnp.full((1, UN), base, f32)
        for bit in range(8):
            result = jnp.where((steps_now >> bit) & 1 == 1, result * base, result)
            base = base * base
        return result

    first_scale = learn_rate / (1.0 - power(beta_one))
    second_scale = 1.0 / (1.0 - power(beta_two))
    for row in range(0, UPDATE_ROWS, 8):
        rows = pl.ds(row, 8)
        clipped = clip_factor * grad_ref[rows]
        new_first = beta_one * first_ref[0, rows] + (1.0 - beta_one) * clipped
        new_second = beta_two * second_ref[0, rows] + (1.0 - beta_two) * clipped * clipped
        change = first_scale * new_first / (jnp.sqrt(new_second * second_scale) + epsilon)
        new_first_ref[0, rows] = new_first
        new_second_ref[0, rows] = new_second
        new_params_ref[0, rows] = params_ref[0, rows] * (1.0 - learn_rate * decay_rate) - change


UPDATE_ROWS = 192


def update(grad_shard, clip_factor, step_counts, params, first_moment, second_moment):
    block = pl.BlockSpec((1, UPDATE_ROWS, UN), lambda i: (0, i, 0))
    return pl.pallas_call(
        update_kernel,
        grid=(DB // UPDATE_ROWS,),
        out_shape=(jax.ShapeDtypeStruct((1, DB, UN), f32),) * 3,
        in_specs=[pl.BlockSpec((UPDATE_ROWS, UN), lambda i: (i, 0)), pl.BlockSpec((1, UN), lambda i: (0, 0)),
                  pl.BlockSpec(memory_space=pltpu.SMEM), block, block, block],
        out_specs=[block] * 3,
        compiler_params=pltpu.CompilerParams(vmem_limit_bytes=16 << 20),
    )(grad_shard, clip_factor, step_counts, params, first_moment, second_moment)


def body(activations, cotangent, params, first_moment, second_moment, step_counts):
    grad_shard, clip_factor = reduced_gradient(activations, pltpu.with_memory_space_constraint(cotangent, pltpu.HBM))
    return update(grad_shard, clip_factor, step_counts, params, first_moment, second_moment)


def solution(mesh):
    in_specs = (
        P("section", "dp", None),
        P("section", "dp", "tensor"),
        P("section", "dp", "tensor"),
        P("section", "dp", "tensor"),
        P("section", "dp", "tensor"),
        P("section"),
    )
    out_specs = (
        P("section", "dp", "tensor"),
        P("section", "dp", "tensor"),
        P("section", "dp", "tensor"),
    )
    return jax.shard_map(body, mesh=mesh, in_specs=in_specs, out_specs=out_specs, check_vma=False)
```

```python
import functools
import math

import jax
import jax.numpy as jnp
from jax import lax
from jax.experimental import pallas as pl
from jax.experimental.pallas import tpu as pltpu
from jax.sharding import PartitionSpec as P

beta_one = 0.9
beta_two = 0.95
learn_rate = 0.05
decay_rate = 0.1
epsilon = 1e-08
clip_scale = 0.25

MESH = pl.DeviceIdType.MESH
f32 = jnp.float32

NY, NZ, DB, UN, TOK = 4, 8, 384, 512, 512
RA, RB = 304, 208
HA, HB = (160, 144), (96, 112)
HA_Z, HB_Y = (176, 128), (32, 176)
TILE = 16
LEVELS = 32766.0

O_AYH = 0
O_AYF = O_AYH + NZ * RA
O_AZH = O_AYF + 2 * NZ * RA
O_AZF = O_AZH + RA
O_BZH = O_AZF + 6 * RA
O_BZF = O_BZH + NY * RB
O_BYH = O_BZF + 6 * NY * RB
O_BYF = O_BYH + RB
ROWS_ALL = O_BYF + 2 * RB
N_PIECES = 76


def piece_ayh(dz, d):
    return dz * 2 + d, O_AYH + dz * RA + d * HA[0], HA[d]


def piece_ayf(dz, d):
    return 16 + dz * 2 + d, O_AYF + (dz * 2 + d) * RA, RA


def piece_azh(d):
    return 32 + d, O_AZH + d * HA_Z[0], HA_Z[d]


def piece_azf(j, d):
    return 34 + (j - 1) * 2 + d, O_AZF + ((j - 1) * 2 + d) * RA, RA


def piece_bzh(dy, d):
    return 40 + dy * 2 + d, O_BZH + dy * RB + d * HB[0], HB[d]


def piece_bzf(dy, j, d):
    return 48 + dy * 6 + (j - 1) * 2 + d, O_BZF + (dy * 6 + (j - 1) * 2 + d) * RB, RB


def piece_byh(d):
    return 72 + d, O_BYH + d * HB_Y[0], HB_Y[d]


def piece_byf(d):
    return 74 + d, O_BYF + d * RB, RB


SCHEDULE = [21, 276, 20, 268, 260, 19, 284, 18, 307, 341, 333, 44, 92, 299, 291, 325, 17, 349, 22, 43, 370, 91, 374, 315, 100, 45, 362, 93, 366, 23, 369, 358, 375, 46, 94, 131, 378, 42, 165, 90, 16, 367, 95, 354, 89, 47, 382, 361, 400, 194, 198, 41, 377, 383, 353, 359, 88, 424, 40, 199, 193, 472, 480, 224]


def firsts(schedule):
    seen, marks = [], []
    for code in schedule:
        block = code % 32
        marks.append(0 if block in seen else len(seen) + 1)
        if block not in seen:
            seen.append(block)
    return seen, marks


BLOCK_ORDER, FIRST_USE = firsts(SCHEDULE)


def pick(table, index):
    values = [jnp.int32(entry) for entry in table]
    step = 1
    while len(values) > 1:
        odd = lax.rem(lax.div(index, step), 2) == 1
        values = [jnp.where(odd, b, a) for a, b in zip(values[::2], values[1::2], strict=True)]
        step *= 2
    return values[0]


EARLY = 2


PEERS_C = [(0, 0, 0, 1)]
PEERS_XY = [(i, j, 0, 0) for i in range(4) for j in range(4) if i or j]
PEERS_Z = [(0, 0, i, 0) for i in range(1, 8)]


def kernel(act_ref, cot_hbm, grad_ref, clip_ref, act, cot_t, total, final, send, recv, send_scale, recv_scale,
           sq_vec, sq_c, sq_xy, sq_z, sq_out, act_sem, send_sem, recv_sem, send_scale_sem, recv_scale_sem,
           norm_send_sem, norm_recv_sem, cot_ref, cot_sem):
    section = lax.axis_index("section")
    dp = lax.axis_index("dp")
    core = lax.axis_index("tensor")
    y, z = lax.div(dp, NZ), lax.rem(dp, NZ)

    def peer(dx, dy, dz, dc):
        return (
            lax.rem(section + dx, 4),
            lax.rem(y + dy, NY) * NZ + lax.rem(z + dz, NZ),
            lax.rem(core + dc, 2),
        )

    def block_columns(dy, dz):
        block = lax.rem(y + dy, NY) * NZ + lax.rem(z + dz, NZ)
        return pl.ds(pl.multiple_of(block * DB, DB), DB)

    barrier = pltpu.get_barrier_semaphore()
    peers = PEERS_C + PEERS_XY + PEERS_Z
    for offset in peers:
        pl.semaphore_signal(barrier, inc=1, device_id=peer(*offset), device_id_type=MESH)

    cot_copy = pltpu.make_async_copy(cot_hbm.at[0], cot_ref, cot_sem)
    cot_copy.start()

    def act_copy(order, offset):
        columns = block_columns(offset // NZ, offset % NZ)
        return pltpu.make_async_copy(act_ref.at[0, :, columns], act.at[:, columns], act_sem.at[order])

    @pl.loop(0, NY * NZ)
    def _(order):
        act_copy(order, pick(BLOCK_ORDER, order)).start()

    cot_copy.wait()
    cot_t[...] = cot_ref[...].T
    def rows_of(offset, count):
        return pl.ds(pl.multiple_of(offset, TILE), count)

    def copies(piece, to):
        number, offset, count = piece
        rows = rows_of(offset, count)
        data = pltpu.make_async_remote_copy(
            src_ref=send.at[rows], dst_ref=recv.at[rows], send_sem=send_sem.at[number], recv_sem=recv_sem.at[number],
            device_id=to, device_id_type=MESH)
        scale = pltpu.make_async_remote_copy(
            src_ref=send_scale.at[number], dst_ref=recv_scale.at[number], send_sem=send_scale_sem.at[number],
            recv_sem=recv_scale_sem.at[number], device_id=to, device_id_type=MESH)
        return data, scale

    nowhere = peer(0, 0, 0, 1)

    def send_off(departures):
        for piece, _, to in departures:
            for copy in copies(piece, to):
                copy.start()

    def step(index, in_a, dy, dz, arrivals, departures):
        start, count = (0, RA) if in_a else (RA, RB)
        total[pl.ds(0, count)] = jnp.dot(
            cot_t[pl.ds(start, count)], act[:, block_columns(dy, dz)], preferred_element_type=f32)
        scales = []
        for piece, _ in arrivals:
            for copy in copies(piece, nowhere):
                copy.wait_recv()
            scales.append(recv_scale[piece[0]])
        top = jnp.zeros((8, DB), f32)
        for row in range(0, count, TILE):
            value = total[pl.ds(row, TILE)]
            for (piece, first), scale in zip(arrivals, scales):
                if first <= row < first + piece[2]:
                    code = recv[rows_of(piece[1] + (row - first), TILE)]
                    value = value + code.astype(jnp.int32).astype(f32) * scale
            if departures:
                if arrivals:
                    total[pl.ds(row, TILE)] = value
                size = jnp.abs(value)
                top = jnp.maximum(top, jnp.maximum(size[:8], size[8:]))
            else:
                final[pl.ds(start + row, TILE)] = value
                square = value * value
                top = top + (square[:8] + square[8:])
        if not departures:
            sq_vec[0 if in_a else 1] = top
            return
        top = jnp.maximum(jnp.max(top, axis=0, keepdims=True), 1e-30)
        inverse = LEVELS / top
        for piece, first, to in departures:
            number, offset, size = piece
            send_scale[number] = top * (1.0 / LEVELS)
            for row in range(0, size, TILE):
                code = jnp.round(total[pl.ds(first + row, TILE)] * inverse)
                send[rows_of(offset + row, TILE)] = code.astype(jnp.int32).astype(jnp.int16)
        if arrivals:
            send_off(departures)
        else:
            pl.when(index >= EARLY)(lambda: send_off(departures))

    y_peer = (peer(0, 1, 0, 0), peer(0, NY - 1, 0, 0))
    z_peer = (peer(0, 0, 1, 0), peer(0, 0, NZ - 1, 0))

    def first_of_a(dz):
        return [(piece_ayh(dz, 0), 0, y_peer[0]), (piece_ayh(dz, 1), HA[0], y_peer[1])]

    def first_of_b(dy):
        return [(piece_bzh(dy, 0), 0, z_peer[0]), (piece_bzh(dy, 1), HB[0], z_peer[1])]

    def z_toward(d):
        return peer(0, 0, 1 + (NZ - 2) * d, 0)

    @pl.loop(0, len(SCHEDULE))
    def _(index):
        @pl.when(index == EARLY)
        def _():
            pl.semaphore_wait(barrier, len(peers))
            for early in SCHEDULE[:EARLY]:
                send_off(first_of_a(early % NZ) if early < 32 else first_of_b(early // NZ % NY))

        entry = pick([code * 64 + mark for code, mark in zip(SCHEDULE, FIRST_USE)], index)
        code, first_use = lax.div(entry, 64), lax.rem(entry, 64)
        kind, offset = lax.div(code, 32), lax.rem(code, 32)
        dy, dz = lax.div(offset, NZ), lax.rem(offset, NZ)

        @pl.when(first_use > 0)
        def _():
            act_copy(first_use - 1, offset).wait()

        kinds = {}

        def when(value):
            return functools.partial(kinds.__setitem__, value)

        @when(0)
        def _():
            step(index, True, dy, dz, [], first_of_a(dz))

        for d in (0, 1):
            @when(1 + d)
            def _(d=d):
                step(index, True, dy, dz, [(piece_ayh(dz, d), d * HA[0])], [(piece_ayf(dz, d), 0, y_peer[d])])

        def summed_over_y():
            return [(piece_ayf(dz, 0), 0), (piece_ayf(dz, 1), 0)]

        @when(3)
        def _():
            step(index, True, dy, dz, summed_over_y(), [
                (piece_azh(0), 0, z_peer[0]), (piece_azh(1), HA_Z[0], z_peer[1])])

        for d in (0, 1):
            @when(4 + d)
            def _(d=d):
                step(index, True, dy, dz, summed_over_y() + [(piece_azh(d), d * HA_Z[0])], [(piece_azf(3, d), 0, z_peer[d])])

        toward = (dz > NZ // 2).astype(jnp.int32)
        hops = jnp.where(dz > NZ // 2, NZ - dz, dz)

        @when(6)
        def _():
            step(index, True, dy, dz, summed_over_y() + [(piece_azf(hops + 1, toward), 0)],
                 [(piece_azf(hops, toward), 0, z_toward(toward))])

        @when(7)
        def _():
            step(index, True, dy, dz, summed_over_y() + [(piece_azf(1, 0), 0), (piece_azf(1, 1), 0)], [])

        @when(8)
        def _():
            step(index, False, dy, dz, [], first_of_b(dy))

        for d in (0, 1):
            @when(9 + d)
            def _(d=d):
                step(index, False, dy, dz, [(piece_bzh(dy, d), d * HB[0])], [(piece_bzf(dy, 3, d), 0, z_peer[d])])

        @when(11)
        def _():
            step(index, False, dy, dz, [(piece_bzf(dy, hops + 1, toward), 0)],
                 [(piece_bzf(dy, hops, toward), 0, z_toward(toward))])

        def summed_over_z():
            return [(piece_bzf(dy, 1, 0), 0), (piece_bzf(dy, 1, 1), 0)]

        @when(12)
        def _():
            step(index, False, dy, dz, summed_over_z(), [
                (piece_byh(0), 0, y_peer[0]), (piece_byh(1), HB_Y[0], y_peer[1])])

        for d in (0, 1):
            @when(13 + d)
            def _(d=d):
                step(index, False, dy, dz, summed_over_z() + [(piece_byh(d), d * HB_Y[0])], [(piece_byf(d), 0, y_peer[d])])

        @when(15)
        def _():
            step(index, False, dy, dz, summed_over_z() + [(piece_byf(0), 0), (piece_byf(1), 0)], [])

        def dispatch(low, high):
            if high - low == 1:
                if low in kinds:
                    kinds[low]()
                return
            middle = (low + high) // 2
            pl.when(kind < middle)(lambda: dispatch(low, middle))
            pl.when(kind >= middle)(lambda: dispatch(middle, high))

        dispatch(0, 16)

    def sent(count, piece):
        @pl.loop(0, count)
        def _(index):
            for copy in copies(piece(index), nowhere):
                copy.wait_send()
    def wait_for_sends():
        for d in (0, 1):
            sent(NZ, lambda i, d=d: piece_ayh(i, d))
            sent(NZ, lambda i, d=d: piece_ayf(i, d))
            sent(1, lambda i, d=d: piece_azh(d))
            sent(3, lambda i, d=d: piece_azf(i + 1, d))
            sent(NY, lambda i, d=d: piece_bzh(i, d))
            for dy in range(NY):
                sent(3, lambda i, d=d, dy=dy: piece_bzf(dy, i + 1, d))
            sent(1, lambda i, d=d: piece_byh(d))
            sent(1, lambda i, d=d: piece_byf(d))

    lanes = jnp.sum(sq_vec[0] + sq_vec[1], axis=0, keepdims=True)
    value = lanes[:, :128] + lanes[:, 128:256] + lanes[:, 256:]
    place = 0
    waiting = []
    for stage, (offsets, slots) in enumerate(((PEERS_C, sq_c), (PEERS_XY, sq_xy), (PEERS_Z, sq_z))):
        sq_out[stage] = value
        exchange = []
        for slot, offset in enumerate(offsets):
            copy = pltpu.make_async_remote_copy(
                src_ref=sq_out.at[stage], dst_ref=slots.at[slot], send_sem=norm_send_sem.at[place],
                recv_sem=norm_recv_sem.at[place], device_id=peer(*offset), device_id_type=MESH)
            copy.start()
            exchange.append(copy)
            place += 1
        if stage == 1:
            wait_for_sends()
        if stage == 2:
            grad_ref[...] = final[...].T
        for copy in exchange:
            copy.wait_recv()
        for slot in range(len(offsets)):
            value = value + slots[slot]
        waiting += exchange
    threshold = clip_scale * math.sqrt(4 * NY * NZ * DB * UN * 2)
    norm = jnp.sqrt(jnp.broadcast_to(jnp.sum(value, axis=1, keepdims=True), (1, UN)))
    clip_ref[...] = jnp.minimum(1.0, threshold / norm)

    for copy in waiting:
        copy.wait_send()


def reduced_gradient(activations, cotangent):
    dma = pltpu.SemaphoreType.DMA
    return pl.pallas_call(
        kernel,
        out_shape=(jax.ShapeDtypeStruct((DB, UN), f32), jax.ShapeDtypeStruct((1, UN), f32)),
        in_specs=[pl.BlockSpec(memory_space=pl.ANY), pl.BlockSpec(memory_space=pltpu.HBM)],
        out_specs=[pl.BlockSpec(memory_space=pltpu.VMEM)] * 2,
        scratch_shapes=[
            pltpu.VMEM((TOK, NY * NZ * DB), jnp.bfloat16),
            pltpu.VMEM((UN, TOK), jnp.bfloat16),
            pltpu.VMEM((RA, DB), f32),
            pltpu.VMEM((UN, DB), f32),
            pltpu.VMEM((ROWS_ALL, DB), jnp.int16),
            pltpu.VMEM((ROWS_ALL, DB), jnp.int16),
            pltpu.VMEM((N_PIECES, 1, DB), f32),
            pltpu.VMEM((N_PIECES, 1, DB), f32),
            pltpu.VMEM((2, 8, DB), f32),
            pltpu.VMEM((1, 1, 128), f32),
            pltpu.VMEM((15, 1, 128), f32),
            pltpu.VMEM((7, 1, 128), f32),
            pltpu.VMEM((3, 1, 128), f32),
            dma((NY * NZ,)),
            dma((N_PIECES,)),
            dma((N_PIECES,)),
            dma((N_PIECES,)),
            dma((N_PIECES,)),
            dma((23,)),
            dma((23,)),
            pltpu.VMEM((TOK, UN), jnp.bfloat16),
            dma(()),
        ],
        compiler_params=pltpu.CompilerParams(collective_id=0, has_side_effects=True, vmem_limit_bytes=46 << 20),
    )(activations, cotangent)


def update_kernel(grad_ref, clip_ref, count_ref, params_ref, first_ref, second_ref, new_params_ref, new_first_ref, new_second_ref):
    clip_factor = clip_ref[...]
    steps_now = jnp.full((1, UN), count_ref[0], jnp.int32)

    def power(base):
        result, base = jnp.ones((1, UN), f32), jnp.full((1, UN), base, f32)
        for bit in range(8):
            result = jnp.where((steps_now >> bit) & 1 == 1, result * base, result)
            base = base * base
        return result

    first_scale = learn_rate / (1.0 - power(beta_one))
    second_scale = 1.0 / (1.0 - power(beta_two))
    for row in range(0, UPDATE_ROWS, 8):
        rows = pl.ds(row, 8)
        clipped = clip_factor * grad_ref[rows]
        new_first = beta_one * first_ref[0, rows] + (1.0 - beta_one) * clipped
        new_second = beta_two * second_ref[0, rows] + (1.0 - beta_two) * clipped * clipped
        change = first_scale * new_first / (jnp.sqrt(new_second * second_scale) + epsilon)
        new_first_ref[0, rows] = new_first
        new_second_ref[0, rows] = new_second
        new_params_ref[0, rows] = params_ref[0, rows] * (1.0 - learn_rate * decay_rate) - change


UPDATE_ROWS = 192


def update(grad_shard, clip_factor, step_counts, params, first_moment, second_moment):
    block = pl.BlockSpec((1, UPDATE_ROWS, UN), lambda i: (0, i, 0))
    return pl.pallas_call(
        update_kernel,
        grid=(DB // UPDATE_ROWS,),
        out_shape=(jax.ShapeDtypeStruct((1, DB, UN), f32),) * 3,
        in_specs=[pl.BlockSpec((UPDATE_ROWS, UN), lambda i: (i, 0)), pl.BlockSpec((1, UN), lambda i: (0, 0)),
                  pl.BlockSpec(memory_space=pltpu.SMEM), block, block, block],
        out_specs=[block] * 3,
        compiler_params=pltpu.CompilerParams(vmem_limit_bytes=16 << 20),
    )(grad_shard, clip_factor, step_counts, params, first_moment, second_moment)


def body(activations, cotangent, params, first_moment, second_moment, step_counts):
    grad_shard, clip_factor = reduced_gradient(activations, pltpu.with_memory_space_constraint(cotangent, pltpu.HBM))
    return update(grad_shard, clip_factor, step_counts, params, first_moment, second_moment)


def solution(mesh):
    in_specs = (
        P("section", "dp", None),
        P("section", "dp", "tensor"),
        P("section", "dp", "tensor"),
        P("section", "dp", "tensor"),
        P("section", "dp", "tensor"),
        P("section"),
    )
    out_specs = (
        P("section", "dp", "tensor"),
        P("section", "dp", "tensor"),
        P("section", "dp", "tensor"),
    )
    return jax.shard_map(body, mesh=mesh, in_specs=in_specs, out_specs=out_specs, check_vma=False)
```

```python
import functools
import math

import jax
import jax.numpy as jnp
from jax import lax
from jax.experimental import pallas as pl
from jax.experimental.pallas import tpu as pltpu
from jax.sharding import PartitionSpec as P

beta_one = 0.9
beta_two = 0.95
learn_rate = 0.05
decay_rate = 0.1
epsilon = 1e-08
clip_scale = 0.25

MESH = pl.DeviceIdType.MESH
f32 = jnp.float32

NY, NZ, DB, UN, TOK = 4, 8, 384, 512, 512
RA, RB = 304, 208
HA, HB = (160, 144), (96, 112)
HA_Z, HB_Y = (176, 128), (32, 176)
TILE = 16
LEVELS = 32766.0

O_AYH = 0
O_AYF = O_AYH + NZ * RA
O_AZH = O_AYF + 2 * NZ * RA
O_AZF = O_AZH + RA
O_BZH = O_AZF + 6 * RA
O_BZF = O_BZH + NY * RB
O_BYH = O_BZF + 6 * NY * RB
O_BYF = O_BYH + RB
ROWS_ALL = O_BYF + 2 * RB
N_PIECES = 76


def piece_ayh(dz, d):
    return dz * 2 + d, O_AYH + dz * RA + d * HA[0], HA[d]


def piece_ayf(dz, d):
    return 16 + dz * 2 + d, O_AYF + (dz * 2 + d) * RA, RA


def piece_azh(d):
    return 32 + d, O_AZH + d * HA_Z[0], HA_Z[d]


def piece_azf(j, d):
    return 34 + (j - 1) * 2 + d, O_AZF + ((j - 1) * 2 + d) * RA, RA


def piece_bzh(dy, d):
    return 40 + dy * 2 + d, O_BZH + dy * RB + d * HB[0], HB[d]


def piece_bzf(dy, j, d):
    return 48 + dy * 6 + (j - 1) * 2 + d, O_BZF + (dy * 6 + (j - 1) * 2 + d) * RB, RB


def piece_byh(d):
    return 72 + d, O_BYH + d * HB_Y[0], HB_Y[d]


def piece_byf(d):
    return 74 + d, O_BYF + d * RB, RB


SCHEDULE = [21, 276, 20, 268, 260, 19, 284, 18, 307, 341, 333, 44, 92, 299, 291, 325, 17, 349, 22, 43, 370, 91, 374, 315, 100, 45, 362, 93, 366, 23, 369, 358, 375, 46, 94, 131, 378, 42, 165, 90, 16, 367, 95, 354, 89, 47, 382, 361, 400, 194, 198, 41, 377, 383, 353, 359, 88, 424, 40, 199, 193, 472, 480, 224]


def firsts(schedule):
    seen, marks = [], []
    for code in schedule:
        block = code % 32
        marks.append(0 if block in seen else len(seen) + 1)
        if block not in seen:
            seen.append(block)
    return seen, marks


BLOCK_ORDER, FIRST_USE = firsts(SCHEDULE)


def pick(table, index):
    values = [jnp.int32(entry) for entry in table]
    step = 1
    while len(values) > 1:
        odd = lax.rem(lax.div(index, step), 2) == 1
        values = [jnp.where(odd, b, a) for a, b in zip(values[::2], values[1::2], strict=True)]
        step *= 2
    return values[0]


EARLY = 2


def farthest_first(offsets):
    return sorted(offsets, key=lambda o: -(min(o[0], 4 - o[0]) + min(o[1], NY - o[1]) + min(o[2], NZ - o[2])))


PEERS_C = [(0, 0, 0, 1)]
PEERS_XY = farthest_first([(i, j, 0, 0) for i in range(4) for j in range(4) if i or j])
PEERS_Z = farthest_first([(0, 0, i, 0) for i in range(1, 8)])


def kernel(act_ref, cot_hbm, grad_ref, clip_ref, act, cot_t, total, final, send, recv, send_scale, recv_scale,
           sq_vec, sq_c, sq_xy, sq_z, sq_out, act_sem, send_sem, recv_sem, send_scale_sem, recv_scale_sem,
           norm_send_sem, norm_recv_sem, cot_ref, cot_sem):
    section = lax.axis_index("section")
    dp = lax.axis_index("dp")
    core = lax.axis_index("tensor")
    y, z = lax.div(dp, NZ), lax.rem(dp, NZ)

    def peer(dx, dy, dz, dc):
        return (
            lax.rem(section + dx, 4),
            lax.rem(y + dy, NY) * NZ + lax.rem(z + dz, NZ),
            lax.rem(core + dc, 2),
        )

    def block_columns(dy, dz):
        block = lax.rem(y + dy, NY) * NZ + lax.rem(z + dz, NZ)
        return pl.ds(pl.multiple_of(block * DB, DB), DB)

    barrier = pltpu.get_barrier_semaphore()
    peers = farthest_first(PEERS_C + PEERS_XY + PEERS_Z)
    for offset in peers:
        pl.semaphore_signal(barrier, inc=1, device_id=peer(*offset), device_id_type=MESH)

    cot_copy = pltpu.make_async_copy(cot_hbm.at[0], cot_ref, cot_sem)
    cot_copy.start()

    def act_copy(order, offset):
        columns = block_columns(offset // NZ, offset % NZ)
        return pltpu.make_async_copy(act_ref.at[0, :, columns], act.at[:, columns], act_sem.at[order])

    @pl.loop(0, NY * NZ)
    def _(order):
        act_copy(order, pick(BLOCK_ORDER, order)).start()

    cot_copy.wait()
    cot_t[...] = cot_ref[...].T
    def rows_of(offset, count):
        return pl.ds(pl.multiple_of(offset, TILE), count)

    def copies(piece, to):
        number, offset, count = piece
        rows = rows_of(offset, count)
        data = pltpu.make_async_remote_copy(
            src_ref=send.at[rows], dst_ref=recv.at[rows], send_sem=send_sem.at[number], recv_sem=recv_sem.at[number],
            device_id=to, device_id_type=MESH)
        scale = pltpu.make_async_remote_copy(
            src_ref=send_scale.at[number], dst_ref=recv_scale.at[number], send_sem=send_scale_sem.at[number],
            recv_sem=recv_scale_sem.at[number], device_id=to, device_id_type=MESH)
        return data, scale

    nowhere = peer(0, 0, 0, 1)

    def send_off(departures):
        for piece, _, to in departures:
            for copy in copies(piece, to):
                copy.start()

    def step(index, in_a, dy, dz, arrivals, departures):
        start, count = (0, RA) if in_a else (RA, RB)
        total[pl.ds(0, count)] = jnp.dot(
            cot_t[pl.ds(start, count)], act[:, block_columns(dy, dz)], preferred_element_type=f32)
        scales = []
        for piece, _ in arrivals:
            for copy in copies(piece, nowhere):
                copy.wait_recv()
            scales.append(recv_scale[piece[0]])
        top = jnp.zeros((8, DB), f32)
        for row in range(0, count, TILE):
            value = total[pl.ds(row, TILE)]
            for (piece, first), scale in zip(arrivals, scales):
                if first <= row < first + piece[2]:
                    code = recv[rows_of(piece[1] + (row - first), TILE)]
                    value = value + code.astype(jnp.int32).astype(f32) * scale
            if departures:
                if arrivals:
                    total[pl.ds(row, TILE)] = value
                size = jnp.abs(value)
                top = jnp.maximum(top, jnp.maximum(size[:8], size[8:]))
            else:
                final[pl.ds(start + row, TILE)] = value
                square = value * value
                top = top + (square[:8] + square[8:])
        if not departures:
            sq_vec[0 if in_a else 1] = top
            return
        top = jnp.maximum(jnp.max(top, axis=0, keepdims=True), 1e-30)
        inverse = LEVELS / top
        for piece, first, to in departures:
            number, offset, size = piece
            send_scale[number] = top * (1.0 / LEVELS)
            for row in range(0, size, TILE):
                code = jnp.round(total[pl.ds(first + row, TILE)] * inverse)
                send[rows_of(offset + row, TILE)] = code.astype(jnp.int32).astype(jnp.int16)
        if arrivals:
            send_off(departures)
        else:
            pl.when(index >= EARLY)(lambda: send_off(departures))

    y_peer = (peer(0, 1, 0, 0), peer(0, NY - 1, 0, 0))
    z_peer = (peer(0, 0, 1, 0), peer(0, 0, NZ - 1, 0))

    def first_of_a(dz):
        return [(piece_ayh(dz, 0), 0, y_peer[0]), (piece_ayh(dz, 1), HA[0], y_peer[1])]

    def first_of_b(dy):
        return [(piece_bzh(dy, 0), 0, z_peer[0]), (piece_bzh(dy, 1), HB[0], z_peer[1])]

    def z_toward(d):
        return peer(0, 0, 1 + (NZ - 2) * d, 0)

    @pl.loop(0, len(SCHEDULE))
    def _(index):
        @pl.when(index == EARLY)
        def _():
            pl.semaphore_wait(barrier, len(peers))
            for early in SCHEDULE[:EARLY]:
                send_off(first_of_a(early % NZ) if early < 32 else first_of_b(early // NZ % NY))

        entry = pick([code * 64 + mark for code, mark in zip(SCHEDULE, FIRST_USE)], index)
        code, first_use = lax.div(entry, 64), lax.rem(entry, 64)
        kind, offset = lax.div(code, 32), lax.rem(code, 32)
        dy, dz = lax.div(offset, NZ), lax.rem(offset, NZ)

        @pl.when(first_use > 0)
        def _():
            act_copy(first_use - 1, offset).wait()

        kinds = {}

        def when(value):
            return functools.partial(kinds.__setitem__, value)

        @when(0)
        def _():
            step(index, True, dy, dz, [], first_of_a(dz))

        for d in (0, 1):
            @when(1 + d)
            def _(d=d):
                step(index, True, dy, dz, [(piece_ayh(dz, d), d * HA[0])], [(piece_ayf(dz, d), 0, y_peer[d])])

        def summed_over_y():
            return [(piece_ayf(dz, 0), 0), (piece_ayf(dz, 1), 0)]

        @when(3)
        def _():
            step(index, True, dy, dz, summed_over_y(), [
                (piece_azh(0), 0, z_peer[0]), (piece_azh(1), HA_Z[0], z_peer[1])])

        for d in (0, 1):
            @when(4 + d)
            def _(d=d):
                step(index, True, dy, dz, summed_over_y() + [(piece_azh(d), d * HA_Z[0])], [(piece_azf(3, d), 0, z_peer[d])])

        toward = (dz > NZ // 2).astype(jnp.int32)
        hops = jnp.where(dz > NZ // 2, NZ - dz, dz)

        @when(6)
        def _():
            step(index, True, dy, dz, summed_over_y() + [(piece_azf(hops + 1, toward), 0)],
                 [(piece_azf(hops, toward), 0, z_toward(toward))])

        @when(7)
        def _():
            step(index, True, dy, dz, summed_over_y() + [(piece_azf(1, 0), 0), (piece_azf(1, 1), 0)], [])

        @when(8)
        def _():
            step(index, False, dy, dz, [], first_of_b(dy))

        for d in (0, 1):
            @when(9 + d)
            def _(d=d):
                step(index, False, dy, dz, [(piece_bzh(dy, d), d * HB[0])], [(piece_bzf(dy, 3, d), 0, z_peer[d])])

        @when(11)
        def _():
            step(index, False, dy, dz, [(piece_bzf(dy, hops + 1, toward), 0)],
                 [(piece_bzf(dy, hops, toward), 0, z_toward(toward))])

        def summed_over_z():
            return [(piece_bzf(dy, 1, 0), 0), (piece_bzf(dy, 1, 1), 0)]

        @when(12)
        def _():
            step(index, False, dy, dz, summed_over_z(), [
                (piece_byh(0), 0, y_peer[0]), (piece_byh(1), HB_Y[0], y_peer[1])])

        for d in (0, 1):
            @when(13 + d)
            def _(d=d):
                step(index, False, dy, dz, summed_over_z() + [(piece_byh(d), d * HB_Y[0])], [(piece_byf(d), 0, y_peer[d])])

        @when(15)
        def _():
            step(index, False, dy, dz, summed_over_z() + [(piece_byf(0), 0), (piece_byf(1), 0)], [])

        def dispatch(low, high):
            if high - low == 1:
                if low in kinds:
                    kinds[low]()
                return
            middle = (low + high) // 2
            pl.when(kind < middle)(lambda: dispatch(low, middle))
            pl.when(kind >= middle)(lambda: dispatch(middle, high))

        dispatch(0, 16)

    def sent(count, piece):
        @pl.loop(0, count)
        def _(index):
            for copy in copies(piece(index), nowhere):
                copy.wait_send()
    def wait_for_sends():
        for d in (0, 1):
            sent(NZ, lambda i, d=d: piece_ayh(i, d))
            sent(NZ, lambda i, d=d: piece_ayf(i, d))
            sent(1, lambda i, d=d: piece_azh(d))
            sent(3, lambda i, d=d: piece_azf(i + 1, d))
            sent(NY, lambda i, d=d: piece_bzh(i, d))
            for dy in range(NY):
                sent(3, lambda i, d=d, dy=dy: piece_bzf(dy, i + 1, d))
            sent(1, lambda i, d=d: piece_byh(d))
            sent(1, lambda i, d=d: piece_byf(d))

    lanes = jnp.sum(sq_vec[0] + sq_vec[1], axis=0, keepdims=True)
    value = lanes[:, :128] + lanes[:, 128:256] + lanes[:, 256:]
    place = 0
    waiting = []
    for stage, (offsets, slots) in enumerate(((PEERS_C, sq_c), (PEERS_XY, sq_xy), (PEERS_Z, sq_z))):
        sq_out[stage] = value
        exchange = []
        for slot, offset in enumerate(offsets):
            copy = pltpu.make_async_remote_copy(
                src_ref=sq_out.at[stage], dst_ref=slots.at[slot], send_sem=norm_send_sem.at[place],
                recv_sem=norm_recv_sem.at[place], device_id=peer(*offset), device_id_type=MESH)
            copy.start()
            exchange.append(copy)
            place += 1
        if stage == 1:
            wait_for_sends()
        if stage == 2:
            grad_ref[...] = final[...].T
        for copy in exchange:
            copy.wait_recv()
        for slot in range(len(offsets)):
            value = value + slots[slot]
        waiting += exchange
    threshold = clip_scale * math.sqrt(4 * NY * NZ * DB * UN * 2)
    norm = jnp.sqrt(jnp.broadcast_to(jnp.sum(value, axis=1, keepdims=True), (1, UN)))
    clip_ref[...] = jnp.minimum(1.0, threshold / norm)

    for copy in waiting:
        copy.wait_send()


def reduced_gradient(activations, cotangent):
    dma = pltpu.SemaphoreType.DMA
    return pl.pallas_call(
        kernel,
        out_shape=(jax.ShapeDtypeStruct((DB, UN), f32), jax.ShapeDtypeStruct((1, UN), f32)),
        in_specs=[pl.BlockSpec(memory_space=pl.ANY), pl.BlockSpec(memory_space=pltpu.HBM)],
        out_specs=[pl.BlockSpec(memory_space=pltpu.VMEM)] * 2,
        scratch_shapes=[
            pltpu.VMEM((TOK, NY * NZ * DB), jnp.bfloat16),
            pltpu.VMEM((UN, TOK), jnp.bfloat16),
            pltpu.VMEM((RA, DB), f32),
            pltpu.VMEM((UN, DB), f32),
            pltpu.VMEM((ROWS_ALL, DB), jnp.int16),
            pltpu.VMEM((ROWS_ALL, DB), jnp.int16),
            pltpu.VMEM((N_PIECES, 1, DB), f32),
            pltpu.VMEM((N_PIECES, 1, DB), f32),
            pltpu.VMEM((2, 8, DB), f32),
            pltpu.VMEM((1, 1, 128), f32),
            pltpu.VMEM((15, 1, 128), f32),
            pltpu.VMEM((7, 1, 128), f32),
            pltpu.VMEM((3, 1, 128), f32),
            dma((NY * NZ,)),
            dma((N_PIECES,)),
            dma((N_PIECES,)),
            dma((N_PIECES,)),
            dma((N_PIECES,)),
            dma((23,)),
            dma((23,)),
            pltpu.VMEM((TOK, UN), jnp.bfloat16),
            dma(()),
        ],
        compiler_params=pltpu.CompilerParams(collective_id=0, has_side_effects=True, vmem_limit_bytes=46 << 20),
    )(activations, cotangent)


def update_kernel(grad_ref, clip_ref, count_ref, params_ref, first_ref, second_ref, new_params_ref, new_first_ref, new_second_ref):
    clip_factor = clip_ref[...]
    steps_now = jnp.full((1, UN), count_ref[0], jnp.int32)

    def power(base):
        result, base = jnp.ones((1, UN), f32), jnp.full((1, UN), base, f32)
        for bit in range(8):
            result = jnp.where((steps_now >> bit) & 1 == 1, result * base, result)
            base = base * base
        return result

    first_scale = learn_rate / (1.0 - power(beta_one))
    second_scale = 1.0 / (1.0 - power(beta_two))
    for row in range(0, UPDATE_ROWS, 8):
        rows = pl.ds(row, 8)
        clipped = clip_factor * grad_ref[rows]
        new_first = beta_one * first_ref[0, rows] + (1.0 - beta_one) * clipped
        new_second = beta_two * second_ref[0, rows] + (1.0 - beta_two) * clipped * clipped
        change = first_scale * new_first / (jnp.sqrt(new_second * second_scale) + epsilon)
        new_first_ref[0, rows] = new_first
        new_second_ref[0, rows] = new_second
        new_params_ref[0, rows] = params_ref[0, rows] * (1.0 - learn_rate * decay_rate) - change


UPDATE_ROWS = 192


def update(grad_shard, clip_factor, step_counts, params, first_moment, second_moment):
    block = pl.BlockSpec((1, UPDATE_ROWS, UN), lambda i: (0, i, 0))
    return pl.pallas_call(
        update_kernel,
        grid=(DB // UPDATE_ROWS,),
        out_shape=(jax.ShapeDtypeStruct((1, DB, UN), f32),) * 3,
        in_specs=[pl.BlockSpec((UPDATE_ROWS, UN), lambda i: (i, 0)), pl.BlockSpec((1, UN), lambda i: (0, 0)),
                  pl.BlockSpec(memory_space=pltpu.SMEM), block, block, block],
        out_specs=[block] * 3,
        compiler_params=pltpu.CompilerParams(vmem_limit_bytes=16 << 20),
    )(grad_shard, clip_factor, step_counts, params, first_moment, second_moment)


def body(activations, cotangent, params, first_moment, second_moment, step_counts):
    grad_shard, clip_factor = reduced_gradient(activations, pltpu.with_memory_space_constraint(cotangent, pltpu.HBM))
    return update(grad_shard, clip_factor, step_counts, params, first_moment, second_moment)


def solution(mesh):
    in_specs = (
        P("section", "dp", None),
        P("section", "dp", "tensor"),
        P("section", "dp", "tensor"),
        P("section", "dp", "tensor"),
        P("section", "dp", "tensor"),
        P("section"),
    )
    out_specs = (
        P("section", "dp", "tensor"),
        P("section", "dp", "tensor"),
        P("section", "dp", "tensor"),
    )
    return jax.shard_map(body, mesh=mesh, in_specs=in_specs, out_specs=out_specs, check_vma=False)
```

```python
import functools
import math

import jax
import jax.numpy as jnp
from jax import lax
from jax.experimental import pallas as pl
from jax.experimental.pallas import tpu as pltpu
from jax.sharding import PartitionSpec as P

beta_one = 0.9
beta_two = 0.95
learn_rate = 0.05
decay_rate = 0.1
epsilon = 1e-08
clip_scale = 0.25

MESH = pl.DeviceIdType.MESH
f32 = jnp.float32

NY, NZ, DB, UN, TOK = 4, 8, 384, 512, 512
RA, RB = 304, 208
HA, HB = (160, 144), (96, 112)
HA_Z, HB_Y = (176, 128), (32, 176)
TILE = 16
LEVELS = 32766.0

O_AYH = 0
O_AYF = O_AYH + NZ * RA
O_AZH = O_AYF + 2 * NZ * RA
O_AZF = O_AZH + RA
O_BZH = O_AZF + 6 * RA
O_BZF = O_BZH + NY * RB
O_BYH = O_BZF + 6 * NY * RB
O_BYF = O_BYH + RB
ROWS_ALL = O_BYF + 2 * RB
N_PIECES = 76


def piece_ayh(dz, d):
    return dz * 2 + d, O_AYH + dz * RA + d * HA[0], HA[d]


def piece_ayf(dz, d):
    return 16 + dz * 2 + d, O_AYF + (dz * 2 + d) * RA, RA


def piece_azh(d):
    return 32 + d, O_AZH + d * HA_Z[0], HA_Z[d]


def piece_azf(j, d):
    return 34 + (j - 1) * 2 + d, O_AZF + ((j - 1) * 2 + d) * RA, RA


def piece_bzh(dy, d):
    return 40 + dy * 2 + d, O_BZH + dy * RB + d * HB[0], HB[d]


def piece_bzf(dy, j, d):
    return 48 + dy * 6 + (j - 1) * 2 + d, O_BZF + (dy * 6 + (j - 1) * 2 + d) * RB, RB


def piece_byh(d):
    return 72 + d, O_BYH + d * HB_Y[0], HB_Y[d]


def piece_byf(d):
    return 74 + d, O_BYF + d * RB, RB


SCHEDULE = [21, 276, 20, 268, 260, 19, 284, 18, 307, 341, 333, 44, 92, 299, 291, 325, 17, 349, 22, 43, 370, 91, 374, 315, 100, 45, 362, 93, 366, 23, 369, 358, 375, 46, 94, 131, 378, 42, 165, 90, 16, 367, 95, 354, 89, 47, 382, 361, 400, 194, 198, 41, 377, 383, 353, 359, 88, 424, 40, 199, 193, 472, 480, 224]


def firsts(schedule):
    seen, marks = [], []
    for code in schedule:
        block = code % 32
        marks.append(0 if block in seen else len(seen) + 1)
        if block not in seen:
            seen.append(block)
    return seen, marks


BLOCK_ORDER, FIRST_USE = firsts(SCHEDULE)


def pick(table, index):
    values = [jnp.int32(entry) for entry in table]
    step = 1
    while len(values) > 1:
        odd = lax.rem(lax.div(index, step), 2) == 1
        values = [jnp.where(odd, b, a) for a, b in zip(values[::2], values[1::2], strict=True)]
        step *= 2
    return values[0]


EARLY = 3


def farthest_first(offsets):
    return sorted(offsets, key=lambda o: -(min(o[0], 4 - o[0]) + min(o[1], NY - o[1]) + min(o[2], NZ - o[2])))


PEERS_C = [(0, 0, 0, 1)]
PEERS_XY = farthest_first([(i, j, 0, 0) for i in range(4) for j in range(4) if i or j])
PEERS_Z = farthest_first([(0, 0, i, 0) for i in range(1, 8)])


def kernel(act_ref, cot_hbm, grad_ref, clip_ref, act, cot_t, total, final, send, recv, send_scale, recv_scale,
           sq_vec, sq_c, sq_xy, sq_z, sq_out, act_sem, send_sem, recv_sem, send_scale_sem, recv_scale_sem,
           norm_send_sem, norm_recv_sem, cot_ref, cot_sem):
    section = lax.axis_index("section")
    dp = lax.axis_index("dp")
    core = lax.axis_index("tensor")
    y, z = lax.div(dp, NZ), lax.rem(dp, NZ)

    def peer(dx, dy, dz, dc):
        return (
            lax.rem(section + dx, 4),
            lax.rem(y + dy, NY) * NZ + lax.rem(z + dz, NZ),
            lax.rem(core + dc, 2),
        )

    def block_columns(dy, dz):
        block = lax.rem(y + dy, NY) * NZ + lax.rem(z + dz, NZ)
        return pl.ds(pl.multiple_of(block * DB, DB), DB)

    barrier = pltpu.get_barrier_semaphore()
    peers = farthest_first(PEERS_C + PEERS_XY + PEERS_Z)
    for offset in peers:
        pl.semaphore_signal(barrier, inc=1, device_id=peer(*offset), device_id_type=MESH)

    cot_copy = pltpu.make_async_copy(cot_hbm.at[0], cot_ref, cot_sem)
    cot_copy.start()

    def act_copy(order, offset):
        columns = block_columns(offset // NZ, offset % NZ)
        return pltpu.make_async_copy(act_ref.at[0, :, columns], act.at[:, columns], act_sem.at[order])

    @pl.loop(0, NY * NZ)
    def _(order):
        act_copy(order, pick(BLOCK_ORDER, order)).start()

    cot_copy.wait()
    cot_t[...] = cot_ref[...].T
    def rows_of(offset, count):
        return pl.ds(pl.multiple_of(offset, TILE), count)

    def copies(piece, to):
        number, offset, count = piece
        rows = rows_of(offset, count)
        data = pltpu.make_async_remote_copy(
            src_ref=send.at[rows], dst_ref=recv.at[rows], send_sem=send_sem.at[number], recv_sem=recv_sem.at[number],
            device_id=to, device_id_type=MESH)
        scale = pltpu.make_async_remote_copy(
            src_ref=send_scale.at[number], dst_ref=recv_scale.at[number], send_sem=send_scale_sem.at[number],
            recv_sem=recv_scale_sem.at[number], device_id=to, device_id_type=MESH)
        return data, scale

    nowhere = peer(0, 0, 0, 1)

    def send_off(departures):
        for piece, _, to in departures:
            for copy in copies(piece, to):
                copy.start()

    def step(index, in_a, dy, dz, arrivals, departures):
        start, count = (0, RA) if in_a else (RA, RB)
        total[pl.ds(0, count)] = jnp.dot(
            cot_t[pl.ds(start, count)], act[:, block_columns(dy, dz)], preferred_element_type=f32)
        scales = []
        for piece, _ in arrivals:
            for copy in copies(piece, nowhere):
                copy.wait_recv()
            scales.append(recv_scale[piece[0]])
        top = jnp.zeros((8, DB), f32)
        for row in range(0, count, TILE):
            value = total[pl.ds(row, TILE)]
            for (piece, first), scale in zip(arrivals, scales):
                if first <= row < first + piece[2]:
                    code = recv[rows_of(piece[1] + (row - first), TILE)]
                    value = value + code.astype(jnp.int32).astype(f32) * scale
            if departures:
                if arrivals:
                    total[pl.ds(row, TILE)] = value
                size = jnp.abs(value)
                top = jnp.maximum(top, jnp.maximum(size[:8], size[8:]))
            else:
                final[pl.ds(start + row, TILE)] = value
                square = value * value
                top = top + (square[:8] + square[8:])
        if not departures:
            sq_vec[0 if in_a else 1] = top
            return
        top = jnp.maximum(jnp.max(top, axis=0, keepdims=True), 1e-30)
        inverse = LEVELS / top
        for piece, first, to in departures:
            number, offset, size = piece
            send_scale[number] = top * (1.0 / LEVELS)
            for row in range(0, size, TILE):
                code = jnp.round(total[pl.ds(first + row, TILE)] * inverse)
                send[rows_of(offset + row, TILE)] = code.astype(jnp.int32).astype(jnp.int16)
        if arrivals:
            send_off(departures)
        else:
            pl.when(index >= EARLY)(lambda: send_off(departures))

    y_peer = (peer(0, 1, 0, 0), peer(0, NY - 1, 0, 0))
    z_peer = (peer(0, 0, 1, 0), peer(0, 0, NZ - 1, 0))

    def first_of_a(dz):
        return [(piece_ayh(dz, 0), 0, y_peer[0]), (piece_ayh(dz, 1), HA[0], y_peer[1])]

    def first_of_b(dy):
        return [(piece_bzh(dy, 0), 0, z_peer[0]), (piece_bzh(dy, 1), HB[0], z_peer[1])]

    def z_toward(d):
        return peer(0, 0, 1 + (NZ - 2) * d, 0)

    @pl.loop(0, len(SCHEDULE))
    def _(index):
        @pl.when(index == EARLY)
        def _():
            pl.semaphore_wait(barrier, len(peers))
            for early in SCHEDULE[:EARLY]:
                send_off(first_of_a(early % NZ) if early < 32 else first_of_b(early // NZ % NY))

        entry = pick([code * 64 + mark for code, mark in zip(SCHEDULE, FIRST_USE)], index)
        code, first_use = lax.div(entry, 64), lax.rem(entry, 64)
        kind, offset = lax.div(code, 32), lax.rem(code, 32)
        dy, dz = lax.div(offset, NZ), lax.rem(offset, NZ)

        @pl.when(first_use > 0)
        def _():
            act_copy(first_use - 1, offset).wait()

        kinds = {}

        def when(value):
            return functools.partial(kinds.__setitem__, value)

        @when(0)
        def _():
            step(index, True, dy, dz, [], first_of_a(dz))

        for d in (0, 1):
            @when(1 + d)
            def _(d=d):
                step(index, True, dy, dz, [(piece_ayh(dz, d), d * HA[0])], [(piece_ayf(dz, d), 0, y_peer[d])])

        def summed_over_y():
            return [(piece_ayf(dz, 0), 0), (piece_ayf(dz, 1), 0)]

        @when(3)
        def _():
            step(index, True, dy, dz, summed_over_y(), [
                (piece_azh(0), 0, z_peer[0]), (piece_azh(1), HA_Z[0], z_peer[1])])

        for d in (0, 1):
            @when(4 + d)
            def _(d=d):
                step(index, True, dy, dz, summed_over_y() + [(piece_azh(d), d * HA_Z[0])], [(piece_azf(3, d), 0, z_peer[d])])

        toward = (dz > NZ // 2).astype(jnp.int32)
        hops = jnp.where(dz > NZ // 2, NZ - dz, dz)

        @when(6)
        def _():
            step(index, True, dy, dz, summed_over_y() + [(piece_azf(hops + 1, toward), 0)],
                 [(piece_azf(hops, toward), 0, z_toward(toward))])

        @when(7)
        def _():
            step(index, True, dy, dz, summed_over_y() + [(piece_azf(1, 0), 0), (piece_azf(1, 1), 0)], [])

        @when(8)
        def _():
            step(index, False, dy, dz, [], first_of_b(dy))

        for d in (0, 1):
            @when(9 + d)
            def _(d=d):
                step(index, False, dy, dz, [(piece_bzh(dy, d), d * HB[0])], [(piece_bzf(dy, 3, d), 0, z_peer[d])])

        @when(11)
        def _():
            step(index, False, dy, dz, [(piece_bzf(dy, hops + 1, toward), 0)],
                 [(piece_bzf(dy, hops, toward), 0, z_toward(toward))])

        def summed_over_z():
            return [(piece_bzf(dy, 1, 0), 0), (piece_bzf(dy, 1, 1), 0)]

        @when(12)
        def _():
            step(index, False, dy, dz, summed_over_z(), [
                (piece_byh(0), 0, y_peer[0]), (piece_byh(1), HB_Y[0], y_peer[1])])

        for d in (0, 1):
            @when(13 + d)
            def _(d=d):
                step(index, False, dy, dz, summed_over_z() + [(piece_byh(d), d * HB_Y[0])], [(piece_byf(d), 0, y_peer[d])])

        @when(15)
        def _():
            step(index, False, dy, dz, summed_over_z() + [(piece_byf(0), 0), (piece_byf(1), 0)], [])

        def dispatch(low, high):
            if high - low == 1:
                if low in kinds:
                    kinds[low]()
                return
            middle = (low + high) // 2
            pl.when(kind < middle)(lambda: dispatch(low, middle))
            pl.when(kind >= middle)(lambda: dispatch(middle, high))

        dispatch(0, 16)

    def sent(count, piece):
        @pl.loop(0, count)
        def _(index):
            for copy in copies(piece(index), nowhere):
                copy.wait_send()
    def wait_for_sends():
        for d in (0, 1):
            sent(NZ, lambda i, d=d: piece_ayh(i, d))
            sent(NZ, lambda i, d=d: piece_ayf(i, d))
            sent(1, lambda i, d=d: piece_azh(d))
            sent(3, lambda i, d=d: piece_azf(i + 1, d))
            sent(NY, lambda i, d=d: piece_bzh(i, d))
            for dy in range(NY):
                sent(3, lambda i, d=d, dy=dy: piece_bzf(dy, i + 1, d))
            sent(1, lambda i, d=d: piece_byh(d))
            sent(1, lambda i, d=d: piece_byf(d))

    lanes = jnp.sum(sq_vec[0] + sq_vec[1], axis=0, keepdims=True)
    value = lanes[:, :128] + lanes[:, 128:256] + lanes[:, 256:]
    place = 0
    waiting = []
    for stage, (offsets, slots) in enumerate(((PEERS_C, sq_c), (PEERS_XY, sq_xy), (PEERS_Z, sq_z))):
        sq_out[stage] = value
        exchange = []
        for slot, offset in enumerate(offsets):
            copy = pltpu.make_async_remote_copy(
                src_ref=sq_out.at[stage], dst_ref=slots.at[slot], send_sem=norm_send_sem.at[place],
                recv_sem=norm_recv_sem.at[place], device_id=peer(*offset), device_id_type=MESH)
            copy.start()
            exchange.append(copy)
            place += 1
        if stage == 1:
            wait_for_sends()
        if stage == 2:
            grad_ref[...] = final[...].T
        for copy in exchange:
            copy.wait_recv()
        for slot in range(len(offsets)):
            value = value + slots[slot]
        waiting += exchange
    threshold = clip_scale * math.sqrt(4 * NY * NZ * DB * UN * 2)
    norm = jnp.sqrt(jnp.broadcast_to(jnp.sum(value, axis=1, keepdims=True), (1, UN)))
    clip_ref[...] = jnp.minimum(1.0, threshold / norm)

    for copy in waiting:
        copy.wait_send()


def reduced_gradient(activations, cotangent):
    dma = pltpu.SemaphoreType.DMA
    return pl.pallas_call(
        kernel,
        out_shape=(jax.ShapeDtypeStruct((DB, UN), f32), jax.ShapeDtypeStruct((1, UN), f32)),
        in_specs=[pl.BlockSpec(memory_space=pl.ANY), pl.BlockSpec(memory_space=pltpu.HBM)],
        out_specs=[pl.BlockSpec(memory_space=pltpu.VMEM)] * 2,
        scratch_shapes=[
            pltpu.VMEM((TOK, NY * NZ * DB), jnp.bfloat16),
            pltpu.VMEM((UN, TOK), jnp.bfloat16),
            pltpu.VMEM((RA, DB), f32),
            pltpu.VMEM((UN, DB), f32),
            pltpu.VMEM((ROWS_ALL, DB), jnp.int16),
            pltpu.VMEM((ROWS_ALL, DB), jnp.int16),
            pltpu.VMEM((N_PIECES, 1, DB), f32),
            pltpu.VMEM((N_PIECES, 1, DB), f32),
            pltpu.VMEM((2, 8, DB), f32),
            pltpu.VMEM((1, 1, 128), f32),
            pltpu.VMEM((15, 1, 128), f32),
            pltpu.VMEM((7, 1, 128), f32),
            pltpu.VMEM((3, 1, 128), f32),
            dma((NY * NZ,)),
            dma((N_PIECES,)),
            dma((N_PIECES,)),
            dma((N_PIECES,)),
            dma((N_PIECES,)),
            dma((23,)),
            dma((23,)),
            pltpu.VMEM((TOK, UN), jnp.bfloat16),
            dma(()),
        ],
        compiler_params=pltpu.CompilerParams(collective_id=0, has_side_effects=True, vmem_limit_bytes=46 << 20),
    )(activations, cotangent)


def update_kernel(grad_ref, clip_ref, count_ref, params_ref, first_ref, second_ref, new_params_ref, new_first_ref, new_second_ref):
    clip_factor = clip_ref[...]
    steps_now = jnp.full((1, UN), count_ref[0], jnp.int32)

    def power(base):
        result, base = jnp.ones((1, UN), f32), jnp.full((1, UN), base, f32)
        for bit in range(8):
            result = jnp.where((steps_now >> bit) & 1 == 1, result * base, result)
            base = base * base
        return result

    first_scale = learn_rate / (1.0 - power(beta_one))
    second_scale = 1.0 / (1.0 - power(beta_two))
    for row in range(0, UPDATE_ROWS, 8):
        rows = pl.ds(row, 8)
        clipped = clip_factor * grad_ref[rows]
        new_first = beta_one * first_ref[0, rows] + (1.0 - beta_one) * clipped
        new_second = beta_two * second_ref[0, rows] + (1.0 - beta_two) * clipped * clipped
        change = first_scale * new_first / (jnp.sqrt(new_second * second_scale) + epsilon)
        new_first_ref[0, rows] = new_first
        new_second_ref[0, rows] = new_second
        new_params_ref[0, rows] = params_ref[0, rows] * (1.0 - learn_rate * decay_rate) - change


UPDATE_ROWS = 192


def update(grad_shard, clip_factor, step_counts, params, first_moment, second_moment):
    block = pl.BlockSpec((1, UPDATE_ROWS, UN), lambda i: (0, i, 0))
    return pl.pallas_call(
        update_kernel,
        grid=(DB // UPDATE_ROWS,),
        out_shape=(jax.ShapeDtypeStruct((1, DB, UN), f32),) * 3,
        in_specs=[pl.BlockSpec((UPDATE_ROWS, UN), lambda i: (i, 0)), pl.BlockSpec((1, UN), lambda i: (0, 0)),
                  pl.BlockSpec(memory_space=pltpu.SMEM), block, block, block],
        out_specs=[block] * 3,
        compiler_params=pltpu.CompilerParams(vmem_limit_bytes=16 << 20),
    )(grad_shard, clip_factor, step_counts, params, first_moment, second_moment)


def body(activations, cotangent, params, first_moment, second_moment, step_counts):
    grad_shard, clip_factor = reduced_gradient(activations, pltpu.with_memory_space_constraint(cotangent, pltpu.HBM))
    return update(grad_shard, clip_factor, step_counts, params, first_moment, second_moment)


def solution(mesh):
    in_specs = (
        P("section", "dp", None),
        P("section", "dp", "tensor"),
        P("section", "dp", "tensor"),
        P("section", "dp", "tensor"),
        P("section", "dp", "tensor"),
        P("section"),
    )
    out_specs = (
        P("section", "dp", "tensor"),
        P("section", "dp", "tensor"),
        P("section", "dp", "tensor"),
    )
    return jax.shard_map(body, mesh=mesh, in_specs=in_specs, out_specs=out_specs, check_vma=False)
```
